32 devices in a mesh: stn: 8 (over y, x, core), tm: 4 (over z).
Axes of the slice: x: 2, y: 2, z: 4, core: 2. Of those that a mesh axis runs over, the one named last changes fastest.
Arguments:
- samples: bfloat16 [512, 524288], P('stn', 'tm'), may hold values from -6 to 6
Outputs:
- visibilities: float32 [32, 2, 512, 512], P(('stn', 'tm'))
The draws below stay inside these ranges and needn't reach their ends.
All inputs are finite; a program needn't handle non-finite values.
Results may differ from the reference program's by a relative error of at most 0.0062.
Values may be sent and summed in bfloat16 or wider, within the bound.
No kernel may reach another device: no remote copies, remote signals or barrier semaphores. Data moves between devices by JAX's collectives and lax.ppermute only.
A program may use at most 256 MiB of HBM per device.

```python
import jax
import jax.numpy as jnp
from jax import lax

IN_DEV = 64
FRAME = 8192
TAPS = 12
INPUTS = 512
FRAMES = 64
SAMPLES = 524288
KEPT = 32
CH_START = 2032
N_STN = 8


def level_of(key, shape, shards, low, high):
    level = 1.0
    for axis_at, parts in shards:
        steps = jax.random.uniform(jax.random.fold_in(jax.random.fold_in(key, 6), axis_at), (parts,), jnp.float32, low / len(shards), high / len(shards))
        level = level * jnp.repeat(jnp.exp(steps), shape[axis_at] // parts).reshape((-1,) + (1,) * (len(shape) - 1 - axis_at))
    return level


def scatter_about(own_key, shape, scale, bound, shards=(), held_as=jnp.bfloat16):
    result = jax.random.normal(own_key, shape, jnp.float32) * scale
    if len(shards) > 0:
        result = level_of(own_key, shape, shards, -0.22, 0.18) * result
    return jnp.clip(result, min=-bound, max=bound).astype(held_as)


def setup_inputs(seed: int = 0) -> dict:
    seeds = jax.random.split(jax.random.key(seed), 2)
    samples = scatter_about(seeds[0], (INPUTS, SAMPLES), 1.0, 6.0, ((0, 8), (1, 4)))
    return dict(samples=samples)


def prototype():
    length = TAPS * FRAME
    place = jnp.arange(length, dtype=jnp.int32).astype(jnp.float32)
    centred = (place - 0.5 * length + 0.5) / FRAME
    window = 0.54 - 0.46 * jnp.cos(2.0 * jnp.pi * place / (length - 1))
    return (jnp.sinc(centred) * window).reshape(TAPS, FRAME)


def transform_table(kept_channels, first_channel):
    sample_index = jnp.arange(FRAME, dtype=jnp.int32)
    column = jnp.arange(2 * kept_channels, dtype=jnp.int32)
    channel = first_channel + column // 2
    phase = (channel[:, None] * sample_index[None, :]) % FRAME
    angle = (2.0 * jnp.pi / FRAME) * phase.astype(jnp.float32)
    scaling = (2.0 / FRAME) ** 0.5
    table = jnp.where((column % 2 == 0)[:, None], jnp.cos(angle), -jnp.sin(angle)) * scaling
    return table.astype(jnp.bfloat16)


def reference(samples):
    prototype_taps = prototype()
    transform = transform_table(KEPT, CH_START)
    margin_frames = TAPS - 1
    grouped = samples.reshape(N_STN, IN_DEV, FRAMES, FRAME)

    def group_spectra(blocks):
        zero_frames = jnp.zeros((IN_DEV, margin_frames, FRAME), blocks.dtype)
        padded = jnp.concatenate([zero_frames, blocks], axis=1)
        running = jnp.zeros((IN_DEV, FRAMES, FRAME), jnp.float32)
        for tap_index in range(TAPS):
            begin = margin_frames - tap_index
            running = running + prototype_taps[tap_index] * padded[:, begin:begin + FRAMES].astype(jnp.float32)
        filtered = running.astype(jnp.bfloat16)
        spectra = lax.dot_general(transform, filtered, (((1,), (2,)), ((), ())),
                                  preferred_element_type=jnp.float32)
        return spectra.astype(jnp.bfloat16)

    spectra_all = lax.map(group_spectra, grouped)

    def correlate(channel):
        picked = lax.dynamic_slice_in_dim(spectra_all, 2 * channel, 2, axis=1)
        ordered = jnp.transpose(picked, (0, 2, 1, 3)).reshape(INPUTS, 2 * FRAMES)
        swapped = jnp.stack([picked[:, 1], -picked[:, 0]], axis=1)
        swapped = jnp.transpose(swapped, (0, 2, 1, 3)).reshape(INPUTS, 2 * FRAMES)
        real_part = jnp.dot(ordered, ordered.T, preferred_element_type=jnp.float32)
        imag_part = jnp.dot(swapped, ordered.T, preferred_element_type=jnp.float32)
        return jnp.stack([real_part, imag_part]) * (1.0 / FRAMES)

    return lax.map(correlate, jnp.arange(KEPT, dtype=jnp.int32))
```

```python
import functools

import jax
import jax.numpy as jnp
import ml_dtypes
import numpy as np
from jax import lax
from jax.experimental import pallas as pl
from jax.experimental.pallas import tpu as pltpu
from jax.sharding import PartitionSpec as P

FRAME = 8192
TAPS = 12
CH_DEV = 1
LANES = 128
SUBLANES = 8
GROUP = 4
DEPTH = 1024


def tables(kept):
    half = kept // 2
    lane = np.arange(FRAME // 2)
    block, inside = lane // LANES, lane % LANES
    even = 2 * LANES * block + np.where(inside % 2 == 0, inside, LANES + inside - 1)
    odd = 2 * LANES * block + np.where(inside % 2 == 0, inside + 1, LANES + inside)
    length = TAPS * FRAME
    place = np.arange(length, dtype=np.float64)
    window = 0.54 - 0.46 * np.cos(2.0 * np.pi * place / (length - 1))
    prototype = (np.sinc((place - 0.5 * length + 0.5) / FRAME) * window).reshape(TAPS, FRAME)
    turned, middle, taps = [], [], []
    for order in (even, odd):
        sign = 1.0 - 2.0 * (order // 2 % 2)
        phase = np.arange(1, half + 1)[:, None] * order[None, :] % FRAME
        angle = 2.0 * np.pi / FRAME * phase
        rows = np.concatenate([np.cos(angle), -np.sin(angle)]) * sign
        turned.append(rows * (2.0 / FRAME) ** 0.5)
        middle.append(np.broadcast_to(sign * (2.0 / FRAME) ** 0.5, (SUBLANES, FRAME // 2)))
        taps.append(np.concatenate([prototype[:, order], np.zeros((2 * SUBLANES - TAPS, FRAME // 2))]))
    rounded = np.concatenate([np.stack(turned), np.stack(middle)], axis=1).astype(ml_dtypes.bfloat16)
    return rounded.astype(np.float32), np.stack(taps).astype(np.float32)


def spectra_kernel(kept, frames, inputs, samples, turned, taps, out, held, turned_v, taps_v, weights, parted, sums,
                   middle, plus, minus, centre, sem, table_sem):
    half = kept // 2
    groups = frames // GROUP
    width = GROUP * FRAME
    columns = GROUP * inputs
    tiles = columns // LANES
    half_rows = frames * inputs // LANES
    copies = [
        pltpu.make_async_copy(samples.at[:, pl.ds(g * width, width)], held.at[g], sem.at[g]) for g in range(groups)
    ]
    table_copies = [
        pltpu.make_async_copy(turned, turned_v, table_sem.at[0]),
        pltpu.make_async_copy(taps, taps_v, table_sem.at[1]),
    ]
    for copy in table_copies:
        copy.start()
    for copy in copies:
        copy.start()
    for ref in (sums, middle, plus, minus, centre):
        ref[...] = jnp.zeros_like(ref)
    for copy in table_copies:
        copy.wait()

    for parity in range(2):

        def weigh(step, carry):
            at = pl.ds(pl.multiple_of(step * 512, 512), 512)
            rows = turned_v[parity, :kept, at]
            for k in range(TAPS):
                weights[parity, k * kept : (k + 1) * kept, at] = (rows * taps_v[parity, k : k + 1, at]).astype(
                    jnp.bfloat16
                )
            weights[parity, TAPS * kept :, at] = (
                turned_v[parity, kept : kept + 1, at] * taps_v[parity, :, at]
            ).astype(jnp.bfloat16)
            return carry

        lax.fori_loop(0, FRAME // 2 // 512, weigh, 0)

    even_lane = lax.broadcasted_iota(jnp.int32, (inputs, LANES), 1) % 2 == 0
    sublane = lax.broadcasted_iota(jnp.int32, (SUBLANES, LANES), 0)

    def group_step(g, carry):
        pltpu.make_async_copy(samples.at[:, pl.ds(0, width)], held.at[g], sem.at[g]).wait()
        totals = [None, None]
        for begin in range(0, FRAME // 2, DEPTH):
            for f in range(GROUP):
                for at in range(begin, begin + DEPTH, LANES):
                    left = held[g, :, f * FRAME + 2 * at : f * FRAME + 2 * at + LANES]
                    right = held[g, :, f * FRAME + 2 * at + LANES : f * FRAME + 2 * at + 2 * LANES]
                    rows = slice(f * inputs, (f + 1) * inputs)
                    parted[0, rows, at : at + LANES] = jnp.where(even_lane, left, pltpu.roll(right, 1, 1))
                    parted[1, rows, at : at + LANES] = jnp.where(even_lane, pltpu.roll(left, LANES - 1, 1), right)
            for parity in range(2):
                product = lax.dot_general(
                    weights[parity, :, begin : begin + DEPTH],
                    parted[parity, :, begin : begin + DEPTH],
                    (((1,), (1,)), ((), ())),
                    preferred_element_type=jnp.float32,
                )
                totals[parity] = product if totals[parity] is None else totals[parity] + product
        for parity in range(2):
            total = totals[parity]
            for k in range(TAPS):
                for tile in range(tiles):
                    lanes = slice(tile * LANES, (tile + 1) * LANES)
                    to = g * tiles + k // 2 + tile
                    sums[parity, k % 2, to] += total[k * kept : (k + 1) * kept, lanes]
                    slab = total[TAPS * kept + k // SUBLANES * SUBLANES :][:SUBLANES, lanes]
                    middle[parity, k % 2, to] += jnp.where(sublane == k % SUBLANES, slab, 0.0)
        return carry

    lax.fori_loop(0, groups, group_step, 0)

    low = lax.broadcasted_iota(jnp.int32, (1, LANES), 1) < LANES // 2

    def joined(ref, parity, tile):
        later = pltpu.roll(ref[parity, 1, tile], LANES // 2, 1)
        if tile == 0:
            earlier = jnp.zeros_like(later)
        else:
            earlier = pltpu.roll(ref[parity, 1, tile - 1], LANES // 2, 1)
        return ref[parity, 0, tile] + jnp.where(low, earlier, later)

    block = 2 * 2 * half_rows
    for tile in range(sums.shape[2]):
        e = joined(sums, 0, tile)
        o = joined(sums, 1, tile)
        e_re, e_im, o_re, o_im = e[:half], e[half:], o[:half], o[half:]
        real = pl.ds(tile, half, stride=block)
        imag = pl.ds(2 * half_rows + tile, half, stride=block)
        plus[real, :] = e_re + o_im
        plus[imag, :] = e_im - o_re
        minus[real, :] = e_re - o_im
        minus[imag, :] = -e_im - o_re
        centre[tile : tile + 1, :] = jnp.sum(joined(middle, 0, tile), axis=0, keepdims=True)
        centre[2 * half_rows + tile : 2 * half_rows + tile + 1, :] = -jnp.sum(
            joined(middle, 1, tile), axis=0, keepdims=True
        )
    for h in range(1, half + 1):
        rows = slice((h - 1) * block, h * block)
        out[half - h] = minus[rows].astype(jnp.bfloat16)
        if h < half:
            out[half + h] = plus[rows].astype(jnp.bfloat16)
    out[half] = centre[...].astype(jnp.bfloat16)


def block_spectra(samples, kept):
    inputs, count = samples.shape
    frames = count // FRAME
    half = kept // 2
    half_rows = frames * inputs // LANES
    turned, taps = tables(kept)
    rows = TAPS * kept + 2 * SUBLANES
    tiles = (frames + TAPS) * inputs // LANES
    any_spec = pl.BlockSpec(memory_space=pl.ANY)
    return pl.pallas_call(
        functools.partial(spectra_kernel, kept, frames, inputs),
        out_shape=jax.ShapeDtypeStruct((kept, 4 * half_rows, LANES), jnp.bfloat16),
        in_specs=[any_spec] * 3,
        out_specs=pl.BlockSpec(memory_space=pltpu.VMEM),
        scratch_shapes=[
            pltpu.VMEM((frames // GROUP, inputs, GROUP * FRAME), jnp.bfloat16),
            pltpu.VMEM(turned.shape, jnp.float32),
            pltpu.VMEM(taps.shape, jnp.float32),
            pltpu.VMEM((2, rows, FRAME // 2), jnp.bfloat16),
            pltpu.VMEM((2, GROUP * inputs, FRAME // 2), jnp.bfloat16),
            pltpu.VMEM((2, 2, tiles, kept, LANES), jnp.float32),
            pltpu.VMEM((2, 2, tiles, SUBLANES, LANES), jnp.float32),
            pltpu.VMEM((half * 4 * half_rows, LANES), jnp.float32),
            pltpu.VMEM((half * 4 * half_rows, LANES), jnp.float32),
            pltpu.VMEM((4 * half_rows, LANES), jnp.float32),
            pltpu.SemaphoreType.DMA((frames // GROUP,)),
            pltpu.SemaphoreType.DMA((2,)),
        ],
        compiler_params=pltpu.CompilerParams(vmem_limit_bytes=60 << 20),
    )(samples, turned, taps)


def correlate_kernel(stations, time_blocks, half_rows, scaling, arrived, out, spectra):
    inputs = stations * LANES // 2

    @pl.when(pl.program_id(0) == 0)
    def _():
        low = lax.broadcasted_iota(jnp.int32, (1, LANES), 1) < LANES // 2

        def own(station, part):
            rows = []
            for z in range(time_blocks):
                here = arrived[station * time_blocks + z, 2 * half_rows * part : 2 * half_rows * (part + 1)]
                total = here[:half_rows].astype(jnp.float32)
                if z > 0:
                    total += last[half_rows:].astype(jnp.float32)
                last = here
                rows.append(total)
            return jnp.concatenate(rows)

        for pair in range(stations // 2):
            parts = []
            for part in range(2):
                first, second = own(2 * pair, part), own(2 * pair + 1, part)
                parts.append(
                    jnp.concatenate(
                        [
                            jnp.where(low, first, pltpu.roll(second, LANES // 2, 1)),
                            jnp.where(low, pltpu.roll(first, LANES // 2, 1), second),
                        ]
                    )
                )
            lanes = slice(pair * LANES, (pair + 1) * LANES)
            spectra[:, lanes] = jnp.concatenate(parts).astype(jnp.bfloat16)
            spectra[:, inputs + pair * LANES : inputs + (pair + 1) * LANES] = jnp.concatenate(
                [parts[1], -parts[0]]
            ).astype(jnp.bfloat16)

    size = out.shape[2]
    begin = pl.multiple_of(pl.program_id(0) * size, LANES)
    out[0, 0] = scaling * lax.dot_general(
        spectra[:, pl.ds(begin, size)],
        spectra[:, :inputs],
        (((0,), (0,)), ((), ())),
        preferred_element_type=jnp.float32,
    )


def correlate(arrived, stations, time_blocks):
    sources, rows, _ = arrived.shape
    half_rows = rows // 4
    inputs = stations * LANES // 2
    size = min(256, inputs)
    per_part = inputs // size
    frames = time_blocks * half_rows * 2
    return pl.pallas_call(
        functools.partial(correlate_kernel, stations, time_blocks, half_rows, 1.0 / frames),
        out_shape=jax.ShapeDtypeStruct((CH_DEV, 2, inputs, inputs), jnp.float32),
        grid=(2 * per_part,),
        in_specs=[pl.BlockSpec(memory_space=pltpu.VMEM)],
        out_specs=pl.BlockSpec((1, 1, size, inputs), lambda i: (0, i // per_part, i % per_part, 0)),
        scratch_shapes=[pltpu.VMEM((2 * frames, 2 * inputs), jnp.bfloat16)],
        compiler_params=pltpu.CompilerParams(vmem_limit_bytes=32 << 20),
    )(arrived)


def on_device(samples):
    stations = lax.axis_size("stn")
    time_blocks = lax.axis_size("tm")
    kept = CH_DEV * stations * time_blocks
    partial = block_spectra(samples, kept)
    arrived = lax.all_to_all(partial, ("stn", "tm"), split_axis=0, concat_axis=0, tiled=True)
    return correlate(arrived, stations, time_blocks)


def solution(mesh):
    return jax.shard_map(
        on_device,
        mesh=mesh,
        in_specs=(P("stn", "tm"),),
        out_specs=P(("stn", "tm"), None, None, None),
        check_vma=False,
    )
```

```python
import functools

import jax
import jax.numpy as jnp
import ml_dtypes
import numpy as np
from jax import lax
from jax.experimental import pallas as pl
from jax.experimental.pallas import tpu as pltpu
from jax.sharding import PartitionSpec as P

FRAME = 8192
TAPS = 12
CH_DEV = 1
LANES = 128
SUBLANES = 8
GROUP = 4
DEPTH = 1024
AHEAD = 5
GROUPS_AHEAD = 2
CORRELATED = 256
NEAR = 256


def tables(kept):
    half = kept // 2
    lane = np.arange(FRAME // 2)
    block, inside = lane // LANES, lane % LANES
    even = 2 * LANES * block + np.where(inside % 2 == 0, inside, LANES + inside - 1)
    odd = 2 * LANES * block + np.where(inside % 2 == 0, (inside - 1) % LANES, LANES + inside)
    length = TAPS * FRAME
    place = np.arange(length, dtype=np.float64)
    window = 0.54 - 0.46 * np.cos(2.0 * np.pi * place / (length - 1))
    prototype = (np.sinc((place - 0.5 * length + 0.5) / FRAME) * window).reshape(TAPS, FRAME)
    turned, middle, taps = [], [], []
    for order in (even, odd):
        sign = 1.0 - 2.0 * (order // 2 % 2)
        phase = np.arange(1, half + 1)[:, None] * order[None, :] % FRAME
        angle = 2.0 * np.pi / FRAME * phase
        rows = np.concatenate([np.cos(angle), -np.sin(angle)]) * sign
        turned.append(rows * (2.0 / FRAME) ** 0.5)
        middle.append(np.broadcast_to(sign * (2.0 / FRAME) ** 0.5, (SUBLANES, FRAME // 2)))
        taps.append(np.concatenate([prototype[:, order], np.zeros((2 * SUBLANES - TAPS, FRAME // 2))]))
    rounded = np.concatenate([np.stack(turned), np.stack(middle)], axis=1).astype(ml_dtypes.bfloat16)
    return rounded, np.stack(taps).astype(np.float32)


def spectra_kernel(kept, frames, inputs, samples, turned, taps, out, held, turned_v, taps_v, weights, added, sums, middle,
                   plus, minus, centre, piece_sem, frame_sem):
    half = kept // 2
    groups = frames // GROUP
    columns = GROUP * inputs
    tiles = columns // LANES
    half_rows = frames * inputs // LANES
    pieces = FRAME // 2 // DEPTH

    def frame_copy(f):
        at = pl.ds(pl.multiple_of(f * FRAME, FRAME), FRAME)
        return pltpu.make_async_copy(samples.at[:, at], held.at[f], frame_sem.at[f])

    def piece_copies(p):
        table = pl.ds(p * DEPTH, DEPTH)
        lanes = pl.ds(p * 2 * DEPTH, 2 * DEPTH)
        yield pltpu.make_async_copy(turned.at[:, :, table], turned_v.at[:, :, table], piece_sem.at[p, GROUP])
        yield pltpu.make_async_copy(taps.at[:, :, table], taps_v.at[:, :, table], piece_sem.at[p, GROUP + 1])
        for f in range(GROUP):
            yield pltpu.make_async_copy(
                samples.at[:, pl.ds(f * FRAME + p * 2 * DEPTH, 2 * DEPTH)], held.at[f, :, lanes], piece_sem.at[p, f]
            )

    def start_piece(p):
        if p < pieces:
            for copy in piece_copies(p):
                copy.start()
        elif p < pieces + frames - GROUP:
            frame_copy(GROUP + p - pieces).start()

    for p in range(AHEAD):
        start_piece(p)
    for ref in (sums, middle, plus, minus, centre):
        ref[...] = jnp.zeros_like(ref)

    even_lane = lax.broadcasted_iota(jnp.int32, (inputs, LANES), 1) % 2 == 0
    sublane = lax.broadcasted_iota(jnp.int32, (SUBLANES, LANES), 0)

    def weigh(at):
        for parity in range(2):
            rows = turned_v[parity, :kept, at].astype(jnp.float32)
            for k in range(TAPS):
                weights[parity, k * kept : (k + 1) * kept, at] = (rows * taps_v[parity, k : k + 1, at]).astype(
                    jnp.bfloat16
                )
            weights[parity, TAPS * kept :, at] = (
                turned_v[parity, kept : kept + 1, at].astype(jnp.float32) * taps_v[parity, :, at]
            ).astype(jnp.bfloat16)

    def parted(g, near):
        even, odd = [], []
        for f in range(GROUP):
            even_lanes, odd_lanes = [], []
            for at in range(near, near + NEAR, LANES):
                left = held[g * GROUP + f, :, 2 * at : 2 * at + LANES]
                right = held[g * GROUP + f, :, 2 * at + LANES : 2 * at + 2 * LANES]
                moved = pltpu.roll(jnp.where(even_lane, right, left), 1, 1)
                even_lanes.append(jnp.where(even_lane, left, moved))
                odd_lanes.append(jnp.where(even_lane, moved, right))
            even.append(jnp.concatenate(even_lanes, axis=1))
            odd.append(jnp.concatenate(odd_lanes, axis=1))
        return jnp.concatenate(even), jnp.concatenate(odd)

    def group_step(g, first):
        if not first:
            for f in range(GROUP):
                frame_copy(g * GROUP + f).wait()

            @pl.when(g + GROUPS_AHEAD < groups)
            def _():
                for f in range(GROUP):
                    frame_copy((g + GROUPS_AHEAD) * GROUP + f).start()

        for p in range(pieces):
            begin = p * DEPTH
            if first:
                for copy in piece_copies(p):
                    copy.wait()
                start_piece(p + AHEAD)
            totals = [None, None]
            for near in range(begin, begin + DEPTH, NEAR):
                at = slice(near, near + NEAR)
                if first:
                    weigh(at)
                for parity, values in enumerate(parted(g, near)):
                    product = lax.dot_general(
                        weights[parity, :, at], values, (((1,), (1,)), ((), ())), preferred_element_type=jnp.float32
                    )
                    totals[parity] = product if totals[parity] is None else totals[parity] + product
            for parity in range(2):
                if p == 0:
                    added[parity] = totals[parity]
                else:
                    added[parity] += totals[parity]
        if first:
            for p in range(pieces + AHEAD, pieces + GROUP * GROUPS_AHEAD):
                start_piece(p)
        for parity in range(2):
            for k in range(TAPS):
                for tile in range(tiles):
                    lanes = slice(tile * LANES, (tile + 1) * LANES)
                    to = g * tiles + k // 2 + tile
                    sums[parity, k % 2, to] += added[parity, k * kept : (k + 1) * kept, lanes]
                    slab = added[parity, pl.ds(TAPS * kept + k // SUBLANES * SUBLANES, SUBLANES), lanes]
                    middle[parity, k % 2, to] += jnp.where(sublane == k % SUBLANES, slab, 0.0)

    group_step(0, True)

    def later_step(g, carry):
        group_step(g, False)
        return carry

    lax.fori_loop(1, groups, later_step, 0)

    low = lax.broadcasted_iota(jnp.int32, (1, LANES), 1) < LANES // 2

    def joined(ref, parity, tile):
        later = pltpu.roll(ref[parity, 1, tile], LANES // 2, 1)
        if tile == 0:
            earlier = jnp.zeros_like(later)
        else:
            earlier = pltpu.roll(ref[parity, 1, tile - 1], LANES // 2, 1)
        return ref[parity, 0, tile] + jnp.where(low, earlier, later)

    block = 2 * 2 * half_rows
    for tile in range(sums.shape[2]):
        e = joined(sums, 0, tile)
        o = joined(sums, 1, tile)
        e_re, e_im, o_re, o_im = e[:half], e[half:], o[:half], o[half:]
        real = pl.ds(tile, half, stride=block)
        imag = pl.ds(2 * half_rows + tile, half, stride=block)
        plus[real, :] = e_re + o_im
        plus[imag, :] = e_im - o_re
        minus[real, :] = e_re - o_im
        minus[imag, :] = -e_im - o_re
        centre[tile : tile + 1, :] = jnp.sum(joined(middle, 0, tile), axis=0, keepdims=True)
        centre[2 * half_rows + tile : 2 * half_rows + tile + 1, :] = -jnp.sum(
            joined(middle, 1, tile), axis=0, keepdims=True
        )
    for h in range(1, half + 1):
        rows = slice((h - 1) * block, h * block)
        out[half - h] = minus[rows].astype(jnp.bfloat16)
        if h < half:
            out[half + h] = plus[rows].astype(jnp.bfloat16)
    out[half] = centre[...].astype(jnp.bfloat16)


def block_spectra(samples, kept):
    inputs, count = samples.shape
    frames = count // FRAME
    half = kept // 2
    half_rows = frames * inputs // LANES
    turned, taps = tables(kept)
    rows = TAPS * kept + 2 * SUBLANES
    tiles = (frames + TAPS) * inputs // LANES
    any_spec = pl.BlockSpec(memory_space=pl.ANY)
    return pl.pallas_call(
        functools.partial(spectra_kernel, kept, frames, inputs),
        out_shape=jax.ShapeDtypeStruct((kept, 4 * half_rows, LANES), jnp.bfloat16),
        in_specs=[any_spec] * 3,
        out_specs=pl.BlockSpec(memory_space=pltpu.VMEM),
        scratch_shapes=[
            pltpu.VMEM((frames, inputs, FRAME), jnp.bfloat16),
            pltpu.VMEM(turned.shape, jnp.bfloat16),
            pltpu.VMEM(taps.shape, jnp.float32),
            pltpu.VMEM((2, rows, FRAME // 2), jnp.bfloat16),
            pltpu.VMEM((2, rows, GROUP * inputs), jnp.float32),
            pltpu.VMEM((2, 2, tiles, kept, LANES), jnp.float32),
            pltpu.VMEM((2, 2, tiles, SUBLANES, LANES), jnp.float32),
            pltpu.VMEM((half * 4 * half_rows, LANES), jnp.float32),
            pltpu.VMEM((half * 4 * half_rows, LANES), jnp.float32),
            pltpu.VMEM((4 * half_rows, LANES), jnp.float32),
            pltpu.SemaphoreType.DMA((FRAME // 2 // DEPTH, GROUP + 2)),
            pltpu.SemaphoreType.DMA((frames,)),
        ],
        compiler_params=pltpu.CompilerParams(vmem_limit_bytes=60 << 20),
    )(samples, turned, taps)


def correlate_kernel(stations, time_blocks, half_rows, scaling, arrived, out, spectra, held, sem):
    inputs = stations * LANES // 2
    low = lax.broadcasted_iota(jnp.int32, (1, LANES), 1) < LANES // 2

    def own(station, part):
        rows = []
        for z in range(time_blocks):
            here = arrived[station * time_blocks + z, 2 * half_rows * part : 2 * half_rows * (part + 1)]
            total = here[:half_rows].astype(jnp.float32)
            if z > 0:
                total += last[half_rows:].astype(jnp.float32)
            last = here
            rows.append(total)
        return jnp.concatenate(rows)

    for pair in range(stations // 2):
        parts = []
        for part in range(2):
            first, second = own(2 * pair, part), own(2 * pair + 1, part)
            parts.append(
                jnp.concatenate(
                    [
                        jnp.where(low, first, pltpu.roll(second, LANES // 2, 1)),
                        jnp.where(low, pltpu.roll(first, LANES // 2, 1), second),
                    ]
                )
            )
        lanes = slice(pair * LANES, (pair + 1) * LANES)
        spectra[:, lanes] = jnp.concatenate(parts).astype(jnp.bfloat16)
        spectra[:, inputs + pair * LANES : inputs + (pair + 1) * LANES] = jnp.concatenate(
            [parts[1], -parts[0]]
        ).astype(jnp.bfloat16)

    size = min(CORRELATED, inputs)
    copies = []
    for part in range(2):
        for begin in range(0, inputs, size):
            rows = slice(begin, begin + size)
            held[part, rows] = scaling * lax.dot_general(
                spectra[:, part * inputs + begin : part * inputs + begin + size],
                spectra[:, :inputs],
                (((0,), (0,)), ((), ())),
                preferred_element_type=jnp.float32,
            )
            copy = pltpu.make_async_copy(held.at[part, rows], out.at[0, part, rows], sem.at[len(copies)])
            copy.start()
            copies.append(copy)
    for copy in copies:
        copy.wait()


def correlate(arrived, stations, time_blocks):
    sources, rows, _ = arrived.shape
    half_rows = rows // 4
    inputs = stations * LANES // 2
    frames = time_blocks * half_rows * 2
    return pl.pallas_call(
        functools.partial(correlate_kernel, stations, time_blocks, half_rows, 1.0 / frames),
        out_shape=jax.ShapeDtypeStruct((CH_DEV, 2, inputs, inputs), jnp.float32),
        in_specs=[pl.BlockSpec(memory_space=pltpu.VMEM)],
        out_specs=pl.BlockSpec(memory_space=pl.ANY),
        scratch_shapes=[
            pltpu.VMEM((2 * frames, 2 * inputs), jnp.bfloat16),
            pltpu.VMEM((2, inputs, inputs), jnp.float32),
            pltpu.SemaphoreType.DMA((2 * inputs // min(CORRELATED, inputs),)),
        ],
        compiler_params=pltpu.CompilerParams(vmem_limit_bytes=32 << 20),
    )(arrived)


def on_device(samples):
    stations = lax.axis_size("stn")
    time_blocks = lax.axis_size("tm")
    kept = CH_DEV * stations * time_blocks
    partial = block_spectra(samples, kept)
    arrived = lax.all_to_all(partial, ("stn", "tm"), split_axis=0, concat_axis=0, tiled=True)
    return correlate(arrived, stations, time_blocks)


def solution(mesh):
    return jax.shard_map(
        on_device,
        mesh=mesh,
        in_specs=(P("stn", "tm"),),
        out_specs=P(("stn", "tm"), None, None, None),
        check_vma=False,
    )
```

```python
import functools

import jax
import jax.numpy as jnp
import ml_dtypes
import numpy as np
from jax import lax
from jax.experimental import pallas as pl
from jax.experimental.pallas import tpu as pltpu
from jax.sharding import PartitionSpec as P

FRAME = 8192
TAPS = 12
CH_DEV = 1
LANES = 128
SUBLANES = 8
GROUP = 4
DEPTH = 1024
AHEAD = 5
GROUPS_AHEAD = 2
CORRELATED = 256
NEAR = 256


def tables(kept):
    half = kept // 2
    lane = np.arange(FRAME // 2)
    block, inside = lane // LANES, lane % LANES
    even = 2 * LANES * block + np.where(inside % 2 == 0, inside, LANES + inside - 1)
    odd = 2 * LANES * block + np.where(inside % 2 == 0, (inside - 1) % LANES, LANES + inside)
    length = TAPS * FRAME
    place = np.arange(length, dtype=np.float64)
    window = 0.54 - 0.46 * np.cos(2.0 * np.pi * place / (length - 1))
    prototype = (np.sinc((place - 0.5 * length + 0.5) / FRAME) * window).reshape(TAPS, FRAME)
    stacks = []
    for order in (even, odd):
        sign = 1.0 - 2.0 * (order // 2 % 2)
        phase = np.arange(1, half + 1)[:, None] * order[None, :] % FRAME
        angle = 2.0 * np.pi / FRAME * phase
        rows = np.concatenate([np.cos(angle), -np.sin(angle)]) * sign
        centre = np.broadcast_to(sign, (SUBLANES, FRAME // 2))
        transform = np.concatenate([rows, centre]) * (2.0 / FRAME) ** 0.5
        transform = transform.astype(ml_dtypes.bfloat16).astype(np.float32)
        none = np.zeros((2 * SUBLANES - TAPS, FRAME // 2))
        stacks.append(np.concatenate([transform, prototype[:, order].astype(np.float32), none]))
    return np.stack(stacks).astype(np.float32)


def spectra_kernel(kept, frames, inputs, samples, table, out, held, table_v, weights, added, sums, middle, plus,
                   minus, centre, piece_sem, frame_sem):
    half = kept // 2
    groups = frames // GROUP
    columns = GROUP * inputs
    tiles = columns // LANES
    half_rows = frames * inputs // LANES
    pieces = FRAME // 2 // DEPTH

    def frame_copy(f):
        at = pl.ds(pl.multiple_of(f * FRAME, FRAME), FRAME)
        return pltpu.make_async_copy(samples.at[:, at], held.at[f], frame_sem.at[f])

    def piece_copies(p):
        at = pl.ds(p * DEPTH, DEPTH)
        lanes = pl.ds(p * 2 * DEPTH, 2 * DEPTH)
        yield pltpu.make_async_copy(table.at[:, :, at], table_v.at[:, :, at], piece_sem.at[p, GROUP])
        for f in range(GROUP):
            yield pltpu.make_async_copy(
                samples.at[:, pl.ds(f * FRAME + p * 2 * DEPTH, 2 * DEPTH)], held.at[f, :, lanes], piece_sem.at[p, f]
            )

    def start_piece(p):
        if p < pieces:
            for copy in piece_copies(p):
                copy.start()
        elif p < pieces + frames - GROUP:
            frame_copy(GROUP + p - pieces).start()

    for p in range(AHEAD):
        start_piece(p)
    for ref in (sums, middle, plus, minus, centre):
        ref[...] = jnp.zeros_like(ref)

    even_lane = lax.broadcasted_iota(jnp.int32, (inputs, LANES), 1) % 2 == 0
    sublane = lax.broadcasted_iota(jnp.int32, (SUBLANES, LANES), 0)

    def weigh(at):
        for parity in range(2):
            rows = table_v[parity, :kept, at]
            taps = table_v[parity, kept + SUBLANES :, at]
            for k in range(TAPS):
                weights[parity, k * kept : (k + 1) * kept, at] = (rows * taps[k : k + 1]).astype(jnp.bfloat16)
            weights[parity, TAPS * kept :, at] = (table_v[parity, kept : kept + 1, at] * taps).astype(jnp.bfloat16)

    def parted(g, near):
        even, odd = [], []
        for f in range(GROUP):
            even_lanes, odd_lanes = [], []
            for at in range(near, near + NEAR, LANES):
                left = held[g * GROUP + f, :, 2 * at : 2 * at + LANES]
                right = held[g * GROUP + f, :, 2 * at + LANES : 2 * at + 2 * LANES]
                moved = pltpu.roll(jnp.where(even_lane, right, left), 1, 1)
                even_lanes.append(jnp.where(even_lane, left, moved))
                odd_lanes.append(jnp.where(even_lane, moved, right))
            even.append(jnp.concatenate(even_lanes, axis=1))
            odd.append(jnp.concatenate(odd_lanes, axis=1))
        return jnp.concatenate(even), jnp.concatenate(odd)

    def group_step(g, first):
        if not first:
            for f in range(GROUP):
                frame_copy(g * GROUP + f).wait()

            @pl.when(g + GROUPS_AHEAD < groups)
            def _():
                for f in range(GROUP):
                    frame_copy((g + GROUPS_AHEAD) * GROUP + f).start()

        for p in range(pieces):
            begin = p * DEPTH
            if first:
                for copy in piece_copies(p):
                    copy.wait()
                start_piece(p + AHEAD)
            totals = [None, None]
            for near in range(begin, begin + DEPTH, NEAR):
                at = slice(near, near + NEAR)
                if first:
                    weigh(at)
                for parity, values in enumerate(parted(g, near)):
                    product = lax.dot_general(
                        weights[parity, :, at], values, (((1,), (1,)), ((), ())), preferred_element_type=jnp.float32
                    )
                    totals[parity] = product if totals[parity] is None else totals[parity] + product
            for parity in range(2):
                if p == 0:
                    added[parity] = totals[parity]
                else:
                    added[parity] += totals[parity]
        if first:
            for p in range(pieces + AHEAD, pieces + GROUP * GROUPS_AHEAD):
                start_piece(p)
        for parity in range(2):
            for k in range(TAPS):
                for tile in range(tiles):
                    lanes = slice(tile * LANES, (tile + 1) * LANES)
                    to = g * tiles + k // 2 + tile
                    sums[parity, k % 2, to] += added[parity, k * kept : (k + 1) * kept, lanes]
                    slab = added[parity, pl.ds(TAPS * kept + k // SUBLANES * SUBLANES, SUBLANES), lanes]
                    middle[parity, k % 2, to] += jnp.where(sublane == k % SUBLANES, slab, 0.0)

    group_step(0, True)

    def later_step(g, carry):
        group_step(g, False)
        return carry

    lax.fori_loop(1, groups, later_step, 0)

    low = lax.broadcasted_iota(jnp.int32, (1, LANES), 1) < LANES // 2

    def joined(ref, parity, tile):
        later = pltpu.roll(ref[parity, 1, tile], LANES // 2, 1)
        if tile == 0:
            earlier = jnp.zeros_like(later)
        else:
            earlier = pltpu.roll(ref[parity, 1, tile - 1], LANES // 2, 1)
        return ref[parity, 0, tile] + jnp.where(low, earlier, later)

    block = 2 * 2 * half_rows
    for tile in range(sums.shape[2]):
        e = joined(sums, 0, tile)
        o = joined(sums, 1, tile)
        e_re, e_im, o_re, o_im = e[:half], e[half:], o[:half], o[half:]
        real = pl.ds(tile, half, stride=block)
        imag = pl.ds(2 * half_rows + tile, half, stride=block)
        plus[real, :] = e_re + o_im
        plus[imag, :] = e_im - o_re
        minus[real, :] = e_re - o_im
        minus[imag, :] = -e_im - o_re
        centre[tile : tile + 1, :] = jnp.sum(joined(middle, 0, tile), axis=0, keepdims=True)
        centre[2 * half_rows + tile : 2 * half_rows + tile + 1, :] = -jnp.sum(
            joined(middle, 1, tile), axis=0, keepdims=True
        )
    for h in range(1, half + 1):
        rows = slice((h - 1) * block, h * block)
        out[half - h] = minus[rows].astype(jnp.bfloat16)
        if h < half:
            out[half + h] = plus[rows].astype(jnp.bfloat16)
    out[half] = centre[...].astype(jnp.bfloat16)


def block_spectra(samples, kept):
    inputs, count = samples.shape
    frames = count // FRAME
    half = kept // 2
    half_rows = frames * inputs // LANES
    table = tables(kept)
    rows = TAPS * kept + 2 * SUBLANES
    tiles = (frames + TAPS) * inputs // LANES
    any_spec = pl.BlockSpec(memory_space=pl.ANY)
    return pl.pallas_call(
        functools.partial(spectra_kernel, kept, frames, inputs),
        out_shape=jax.ShapeDtypeStruct((kept, 4 * half_rows, LANES), jnp.bfloat16),
        in_specs=[any_spec] * 2,
        out_specs=pl.BlockSpec(memory_space=pltpu.VMEM),
        scratch_shapes=[
            pltpu.VMEM((frames, inputs, FRAME), jnp.bfloat16),
            pltpu.VMEM(table.shape, jnp.float32),
            pltpu.VMEM((2, rows, FRAME // 2), jnp.bfloat16),
            pltpu.VMEM((2, rows, GROUP * inputs), jnp.float32),
            pltpu.VMEM((2, 2, tiles, kept, LANES), jnp.float32),
            pltpu.VMEM((2, 2, tiles, SUBLANES, LANES), jnp.float32),
            pltpu.VMEM((half * 4 * half_rows, LANES), jnp.float32),
            pltpu.VMEM((half * 4 * half_rows, LANES), jnp.float32),
            pltpu.VMEM((4 * half_rows, LANES), jnp.float32),
            pltpu.SemaphoreType.DMA((FRAME // 2 // DEPTH, GROUP + 1)),
            pltpu.SemaphoreType.DMA((frames,)),
        ],
        compiler_params=pltpu.CompilerParams(vmem_limit_bytes=(52 if rows <= 512 else 63) << 20),
    )(samples, table)


def correlate_kernel(stations, time_blocks, half_rows, scaling, arrived, out, spectra, held, sem):
    inputs = stations * LANES // 2
    low = lax.broadcasted_iota(jnp.int32, (1, LANES), 1) < LANES // 2

    def own(station, part):
        rows = []
        for z in range(time_blocks):
            here = arrived[station * time_blocks + z, 2 * half_rows * part : 2 * half_rows * (part + 1)]
            total = here[:half_rows].astype(jnp.float32)
            if z > 0:
                total += last[half_rows:].astype(jnp.float32)
            last = here
            rows.append(total)
        return jnp.concatenate(rows)

    for pair in range(stations // 2):
        parts = []
        for part in range(2):
            first, second = own(2 * pair, part), own(2 * pair + 1, part)
            parts.append(
                jnp.concatenate(
                    [
                        jnp.where(low, first, pltpu.roll(second, LANES // 2, 1)),
                        jnp.where(low, pltpu.roll(first, LANES // 2, 1), second),
                    ]
                )
            )
        lanes = slice(pair * LANES, (pair + 1) * LANES)
        spectra[:, lanes] = jnp.concatenate(parts).astype(jnp.bfloat16)
        spectra[:, inputs + pair * LANES : inputs + (pair + 1) * LANES] = jnp.concatenate(
            [parts[1], -parts[0]]
        ).astype(jnp.bfloat16)

    size = min(CORRELATED, inputs)
    copies = []
    for part in range(2):
        for begin in range(0, inputs, size):
            rows = slice(begin, begin + size)
            held[part, rows] = scaling * lax.dot_general(
                spectra[:, part * inputs + begin : part * inputs + begin + size],
                spectra[:, :inputs],
                (((0,), (0,)), ((), ())),
                preferred_element_type=jnp.float32,
            )
            copy = pltpu.make_async_copy(held.at[part, rows], out.at[0, part, rows], sem.at[len(copies)])
            copy.start()
            copies.append(copy)
    for copy in copies:
        copy.wait()


def correlate(arrived, stations, time_blocks):
    sources, rows, _ = arrived.shape
    half_rows = rows // 4
    inputs = stations * LANES // 2
    frames = time_blocks * half_rows * 2
    return pl.pallas_call(
        functools.partial(correlate_kernel, stations, time_blocks, half_rows, 1.0 / frames),
        out_shape=jax.ShapeDtypeStruct((CH_DEV, 2, inputs, inputs), jnp.float32),
        in_specs=[pl.BlockSpec(memory_space=pltpu.VMEM)],
        out_specs=pl.BlockSpec(memory_space=pl.ANY),
        scratch_shapes=[
            pltpu.VMEM((2 * frames, 2 * inputs), jnp.bfloat16),
            pltpu.VMEM((2, inputs, inputs), jnp.float32),
            pltpu.SemaphoreType.DMA((2 * inputs // min(CORRELATED, inputs),)),
        ],
        compiler_params=pltpu.CompilerParams(vmem_limit_bytes=32 << 20),
    )(arrived)


def on_device(samples):
    stations = lax.axis_size("stn")
    time_blocks = lax.axis_size("tm")
    kept = CH_DEV * stations * time_blocks
    partial = block_spectra(samples, kept)
    arrived = lax.all_to_all(partial, ("stn", "tm"), split_axis=0, concat_axis=0, tiled=True)
    return correlate(arrived, stations, time_blocks)


def solution(mesh):
    return jax.shard_map(
        on_device,
        mesh=mesh,
        in_specs=(P("stn", "tm"),),
        out_specs=P(("stn", "tm"), None, None, None),
        check_vma=False,
    )
```

```python
import functools

import jax
import jax.numpy as jnp
import ml_dtypes
import numpy as np
from jax import lax
from jax.experimental import pallas as pl
from jax.experimental.pallas import tpu as pltpu
from jax.sharding import PartitionSpec as P

FRAME = 8192
TAPS = 12
CH_DEV = 1
LANES = 128
SUBLANES = 8
GROUP = 4
PIECES = (0, 1024, 2048)
AHEAD = 8
BY_PIECE = 1
CORRELATED = 256
NEAR = 256


def tables(kept):
    half = kept // 2
    lane = np.arange(FRAME // 2)
    block, inside = lane // LANES, lane % LANES
    even = 2 * LANES * block + np.where(inside % 2 == 0, inside, LANES + inside - 1)
    odd = 2 * LANES * block + np.where(inside % 2 == 0, (inside - 1) % LANES, LANES + inside)
    length = TAPS * FRAME
    place = np.arange(length, dtype=np.float64)
    window = 0.54 - 0.46 * np.cos(2.0 * np.pi * place / (length - 1))
    prototype = (np.sinc((place - 0.5 * length + 0.5) / FRAME) * window).reshape(TAPS, FRAME)
    stacks = []
    for order in (even, odd):
        sign = 1.0 - 2.0 * (order // 2 % 2)
        phase = np.arange(1, half + 1)[:, None] * order[None, :] % FRAME
        angle = 2.0 * np.pi / FRAME * phase
        rows = np.concatenate([np.cos(angle), -np.sin(angle)]) * sign
        centre = np.broadcast_to(sign, (SUBLANES, FRAME // 2))
        transform = np.concatenate([rows, centre]) * (2.0 / FRAME) ** 0.5
        transform = transform.astype(ml_dtypes.bfloat16).astype(np.float32)
        none = np.zeros((2 * SUBLANES - TAPS, FRAME // 2))
        stacks.append(np.concatenate([transform, prototype[:, order].astype(np.float32), none]))
    return np.stack(stacks).astype(np.float32)


def spectra_kernel(kept, frames, inputs, samples, table, out, held, table_v, weights, added, sums, middle, plus,
                   minus, centre, piece_sem, frame_sem):
    half = kept // 2
    groups = frames // GROUP
    columns = GROUP * inputs
    tiles = columns // LANES
    half_rows = frames * inputs // LANES
    edges = PIECES + (FRAME // 2,)
    pieces = len(PIECES)

    def frame_copy(f):
        at = pl.ds(pl.multiple_of(f * FRAME, FRAME), FRAME)
        return pltpu.make_async_copy(samples.at[:, at], held.at[f], frame_sem.at[f])

    def piece_copies(g, p):
        begin, size = edges[p], edges[p + 1] - edges[p]
        lanes = pl.ds(2 * begin, 2 * size)
        sems = piece_sem.at[g * pieces + p]
        if g == 0:
            at = pl.ds(begin, size)
            yield pltpu.make_async_copy(table.at[:, :, at], table_v.at[:, :, at], sems.at[GROUP])
        for f in range(g * GROUP, (g + 1) * GROUP):
            yield pltpu.make_async_copy(
                samples.at[:, pl.ds(f * FRAME + 2 * begin, 2 * size)], held.at[f, :, lanes], sems.at[f - g * GROUP]
            )

    def start(step):
        if step < BY_PIECE * pieces:
            for copy in piece_copies(step // pieces, step % pieces):
                copy.start()
        elif step - BY_PIECE * pieces < frames - BY_PIECE * GROUP:
            frame_copy(BY_PIECE * GROUP + step - BY_PIECE * pieces).start()

    for step in range(AHEAD):
        start(step)
    for ref in (sums, middle, plus, minus, centre):
        ref[...] = jnp.zeros_like(ref)

    even_lane = lax.broadcasted_iota(jnp.int32, (inputs, LANES), 1) % 2 == 0
    sublane = lax.broadcasted_iota(jnp.int32, (SUBLANES, LANES), 0)

    def weigh(at):
        for parity in range(2):
            rows = table_v[parity, :kept, at]
            taps = table_v[parity, kept + SUBLANES :, at]
            for k in range(TAPS):
                weights[parity, k * kept : (k + 1) * kept, at] = (rows * taps[k : k + 1]).astype(jnp.bfloat16)
            weights[parity, TAPS * kept :, at] = (table_v[parity, kept : kept + 1, at] * taps).astype(jnp.bfloat16)

    def parted(g, near):
        even, odd = [], []
        for f in range(GROUP):
            even_lanes, odd_lanes = [], []
            for at in range(near, near + NEAR, LANES):
                left = held[g * GROUP + f, :, 2 * at : 2 * at + LANES]
                right = held[g * GROUP + f, :, 2 * at + LANES : 2 * at + 2 * LANES]
                moved = pltpu.roll(jnp.where(even_lane, right, left), 1, 1)
                even_lanes.append(jnp.where(even_lane, left, moved))
                odd_lanes.append(jnp.where(even_lane, moved, right))
            even.append(jnp.concatenate(even_lanes, axis=1))
            odd.append(jnp.concatenate(odd_lanes, axis=1))
        return jnp.concatenate(even), jnp.concatenate(odd)

    def group_step(g, by_piece, first=False):
        if not by_piece:
            for f in range(GROUP):
                frame_copy(g * GROUP + f).wait()
        for p in range(pieces):
            if by_piece:
                for copy in piece_copies(g, p):
                    copy.wait()
                start(g * pieces + p + AHEAD)
            totals = [None, None]
            for near in range(edges[p], edges[p + 1], NEAR):
                at = slice(near, near + NEAR)
                if first:
                    weigh(at)
                for parity, values in enumerate(parted(g, near)):
                    product = lax.dot_general(
                        weights[parity, :, at], values, (((1,), (1,)), ((), ())), preferred_element_type=jnp.float32
                    )
                    totals[parity] = product if totals[parity] is None else totals[parity] + product
            for parity in range(2):
                if p == 0:
                    added[parity] = totals[parity]
                else:
                    added[parity] += totals[parity]
        for parity in range(2):
            for k in range(TAPS):
                for tile in range(tiles):
                    lanes = slice(tile * LANES, (tile + 1) * LANES)
                    to = g * tiles + k // 2 + tile
                    sums[parity, k % 2, to] += added[parity, k * kept : (k + 1) * kept, lanes]
                    slab = added[parity, pl.ds(TAPS * kept + k // SUBLANES * SUBLANES, SUBLANES), lanes]
                    middle[parity, k % 2, to] += jnp.where(sublane == k % SUBLANES, slab, 0.0)

    for g in range(BY_PIECE):
        group_step(g, True, g == 0)
    for step in range(BY_PIECE * pieces + AHEAD, BY_PIECE * pieces + frames - BY_PIECE * GROUP):
        start(step)

    def later_step(g, carry):
        group_step(g, False)
        return carry

    lax.fori_loop(BY_PIECE, groups, later_step, 0)

    low = lax.broadcasted_iota(jnp.int32, (1, LANES), 1) < LANES // 2

    def joined(ref, parity):
        earlier = None
        for tile in range(ref.shape[2]):
            later = pltpu.roll(ref[parity, 1, tile], LANES // 2, 1)
            yield ref[parity, 0, tile] + jnp.where(low, 0.0 if earlier is None else earlier, later)
            earlier = later

    block = 2 * 2 * half_rows
    both = [joined(sums, 0), joined(sums, 1), joined(middle, 0), joined(middle, 1)]
    for tile, (e, o, e_mid, o_mid) in enumerate(zip(*both)):
        e_re, e_im, o_re, o_im = e[:half], e[half:], o[:half], o[half:]
        real = pl.ds(tile, half, stride=block)
        imag = pl.ds(2 * half_rows + tile, half, stride=block)
        plus[real, :] = e_re + o_im
        plus[imag, :] = e_im - o_re
        minus[real, :] = e_re - o_im
        minus[imag, :] = -e_im - o_re
        centre[tile : tile + 1, :] = jnp.sum(e_mid, axis=0, keepdims=True)
        centre[2 * half_rows + tile : 2 * half_rows + tile + 1, :] = -jnp.sum(o_mid, axis=0, keepdims=True)
    for h in range(1, half + 1):
        rows = slice((h - 1) * block, h * block)
        out[half - h] = minus[rows].astype(jnp.bfloat16)
        if h < half:
            out[half + h] = plus[rows].astype(jnp.bfloat16)
    out[half] = centre[...].astype(jnp.bfloat16)


def block_spectra(samples, kept):
    inputs, count = samples.shape
    frames = count // FRAME
    half = kept // 2
    half_rows = frames * inputs // LANES
    table = tables(kept)
    rows = TAPS * kept + 2 * SUBLANES
    tiles = (frames + TAPS) * inputs // LANES
    any_spec = pl.BlockSpec(memory_space=pl.ANY)
    return pl.pallas_call(
        functools.partial(spectra_kernel, kept, frames, inputs),
        out_shape=jax.ShapeDtypeStruct((kept, 4 * half_rows, LANES), jnp.bfloat16),
        in_specs=[any_spec] * 2,
        out_specs=pl.BlockSpec(memory_space=pltpu.VMEM),
        scratch_shapes=[
            pltpu.VMEM((frames, inputs, FRAME), jnp.bfloat16),
            pltpu.VMEM(table.shape, jnp.float32),
            pltpu.VMEM((2, rows, FRAME // 2), jnp.bfloat16),
            pltpu.VMEM((2, rows, GROUP * inputs), jnp.float32),
            pltpu.VMEM((2, 2, tiles, kept, LANES), jnp.float32),
            pltpu.VMEM((2, 2, tiles, SUBLANES, LANES), jnp.float32),
            pltpu.VMEM((half * 4 * half_rows, LANES), jnp.float32),
            pltpu.VMEM((half * 4 * half_rows, LANES), jnp.float32),
            pltpu.VMEM((4 * half_rows, LANES), jnp.float32),
            pltpu.SemaphoreType.DMA((BY_PIECE * len(PIECES), GROUP + 1)),
            pltpu.SemaphoreType.DMA((frames,)),
        ],
        compiler_params=pltpu.CompilerParams(vmem_limit_bytes=(52 if rows <= 512 else 63) << 20),
    )(samples, table)


def correlate_kernel(stations, time_blocks, half_rows, scaling, arrived, out, spectra, held, sem):
    inputs = stations * LANES // 2
    low = lax.broadcasted_iota(jnp.int32, (1, LANES), 1) < LANES // 2

    def own(station, part):
        rows = []
        for z in range(time_blocks):
            here = arrived[station * time_blocks + z, 2 * half_rows * part : 2 * half_rows * (part + 1)]
            total = here[:half_rows].astype(jnp.float32)
            if z > 0:
                total += last[half_rows:].astype(jnp.float32)
            last = here
            rows.append(total)
        return jnp.concatenate(rows)

    for pair in range(stations // 2):
        parts = []
        for part in range(2):
            first, second = own(2 * pair, part), own(2 * pair + 1, part)
            parts.append(
                jnp.concatenate(
                    [
                        jnp.where(low, first, pltpu.roll(second, LANES // 2, 1)),
                        jnp.where(low, pltpu.roll(first, LANES // 2, 1), second),
                    ]
                )
            )
        lanes = slice(pair * LANES, (pair + 1) * LANES)
        spectra[:, lanes] = jnp.concatenate(parts).astype(jnp.bfloat16)
        spectra[:, inputs + pair * LANES : inputs + (pair + 1) * LANES] = jnp.concatenate(
            [parts[1], -parts[0]]
        ).astype(jnp.bfloat16)

    size = min(CORRELATED, inputs)
    copies = []
    for part in range(2):
        for begin in range(0, inputs, size):
            rows = slice(begin, begin + size)
            held[part, rows] = scaling * lax.dot_general(
                spectra[:, part * inputs + begin : part * inputs + begin + size],
                spectra[:, :inputs],
                (((0,), (0,)), ((), ())),
                preferred_element_type=jnp.float32,
            )
            copy = pltpu.make_async_copy(held.at[part, rows], out.at[0, part, rows], sem.at[len(copies)])
            copy.start()
            copies.append(copy)
    for copy in copies:
        copy.wait()


def correlate(arrived, stations, time_blocks):
    sources, rows, _ = arrived.shape
    half_rows = rows // 4
    inputs = stations * LANES // 2
    frames = time_blocks * half_rows * 2
    return pl.pallas_call(
        functools.partial(correlate_kernel, stations, time_blocks, half_rows, 1.0 / frames),
        out_shape=jax.ShapeDtypeStruct((CH_DEV, 2, inputs, inputs), jnp.float32),
        in_specs=[pl.BlockSpec(memory_space=pltpu.VMEM)],
        out_specs=pl.BlockSpec(memory_space=pl.ANY),
        scratch_shapes=[
            pltpu.VMEM((2 * frames, 2 * inputs), jnp.bfloat16),
            pltpu.VMEM((2, inputs, inputs), jnp.float32),
            pltpu.SemaphoreType.DMA((2 * inputs // min(CORRELATED, inputs),)),
        ],
        compiler_params=pltpu.CompilerParams(vmem_limit_bytes=32 << 20),
    )(arrived)


def on_device(samples):
    stations = lax.axis_size("stn")
    time_blocks = lax.axis_size("tm")
    kept = CH_DEV * stations * time_blocks
    partial = block_spectra(samples, kept)
    arrived = lax.all_to_all(partial, ("stn", "tm"), split_axis=0, concat_axis=0, tiled=True)
    return correlate(arrived, stations, time_blocks)


def solution(mesh):
    return jax.shard_map(
        on_device,
        mesh=mesh,
        in_specs=(P("stn", "tm"),),
        out_specs=P(("stn", "tm"), None, None, None),
        check_vma=False,
    )
```

```python
import functools

import jax
import jax.numpy as jnp
import ml_dtypes
import numpy as np
from jax import lax
from jax.experimental import pallas as pl
from jax.experimental.pallas import tpu as pltpu
from jax.sharding import PartitionSpec as P

FRAME = 8192
TAPS = 12
CH_DEV = 1
LANES = 128
SUBLANES = 8
GROUP = 4
PIECES = (0, 1024, 2048)
AHEAD = 8
BY_PIECE = 1
CORRELATED = 256
NEAR = 256


def tables(kept):
    half = kept // 2
    lane = np.arange(FRAME // 2)
    block, inside = lane // LANES, lane % LANES
    even = 2 * LANES * block + np.where(inside % 2 == 0, inside, LANES + inside - 1)
    odd = 2 * LANES * block + np.where(inside % 2 == 0, (inside - 1) % LANES, LANES + inside)
    length = TAPS * FRAME
    place = np.arange(length, dtype=np.float64)
    window = 0.54 - 0.46 * np.cos(2.0 * np.pi * place / (length - 1))
    prototype = (np.sinc((place - 0.5 * length + 0.5) / FRAME) * window).reshape(TAPS, FRAME)
    stacks = []
    for order in (even, odd):
        sign = 1.0 - 2.0 * (order // 2 % 2)
        phase = np.arange(1, half + 1)[:, None] * order[None, :] % FRAME
        angle = 2.0 * np.pi / FRAME * phase
        rows = np.concatenate([np.cos(angle), -np.sin(angle)]) * sign
        centre = np.broadcast_to(sign, (SUBLANES, FRAME // 2))
        transform = np.concatenate([rows, centre]) * (2.0 / FRAME) ** 0.5
        transform = transform.astype(ml_dtypes.bfloat16).astype(np.float32)
        none = np.zeros((2 * SUBLANES - TAPS, FRAME // 2))
        stacks.append(np.concatenate([transform, prototype[:, order].astype(np.float32), none]))
    return np.stack(stacks).astype(np.float32)


def spectra_kernel(kept, frames, inputs, samples, table, out, held, table_v, weights, added, sums, middle, centre,
                   piece_sem, frame_sem):
    half = kept // 2
    groups = frames // GROUP
    columns = GROUP * inputs
    tiles = columns // LANES
    half_rows = frames * inputs // LANES
    edges = PIECES + (FRAME // 2,)
    pieces = len(PIECES)

    def frame_copy(f):
        at = pl.ds(pl.multiple_of(f * FRAME, FRAME), FRAME)
        return pltpu.make_async_copy(samples.at[:, at], held.at[f], frame_sem.at[f])

    def piece_copies(g, p):
        begin, size = edges[p], edges[p + 1] - edges[p]
        lanes = pl.ds(2 * begin, 2 * size)
        sems = piece_sem.at[g * pieces + p]
        if g == 0:
            at = pl.ds(begin, size)
            yield pltpu.make_async_copy(table.at[:, :, at], table_v.at[:, :, at], sems.at[GROUP])
        for f in range(g * GROUP, (g + 1) * GROUP):
            yield pltpu.make_async_copy(
                samples.at[:, pl.ds(f * FRAME + 2 * begin, 2 * size)], held.at[f, :, lanes], sems.at[f - g * GROUP]
            )

    def start(step):
        if step < BY_PIECE * pieces:
            for copy in piece_copies(step // pieces, step % pieces):
                copy.start()
        elif step - BY_PIECE * pieces < frames - BY_PIECE * GROUP:
            frame_copy(BY_PIECE * GROUP + step - BY_PIECE * pieces).start()

    for step in range(AHEAD):
        start(step)
    for ref in (sums, middle, centre):
        ref[...] = jnp.zeros_like(ref)

    even_lane = lax.broadcasted_iota(jnp.int32, (inputs, LANES), 1) % 2 == 0
    sublane = lax.broadcasted_iota(jnp.int32, (SUBLANES, LANES), 0)

    def weigh(at):
        for parity in range(2):
            rows = table_v[parity, :kept, at]
            taps = table_v[parity, kept + SUBLANES :, at]
            for k in range(TAPS):
                weights[parity, k * kept : (k + 1) * kept, at] = (rows * taps[k : k + 1]).astype(jnp.bfloat16)
            weights[parity, TAPS * kept :, at] = (table_v[parity, kept : kept + 1, at] * taps).astype(jnp.bfloat16)

    def parted(g, near):
        even, odd = [], []
        for f in range(GROUP):
            even_lanes, odd_lanes = [], []
            for at in range(near, near + NEAR, LANES):
                left = held[g * GROUP + f, :, 2 * at : 2 * at + LANES]
                right = held[g * GROUP + f, :, 2 * at + LANES : 2 * at + 2 * LANES]
                moved = pltpu.roll(jnp.where(even_lane, right, left), 1, 1)
                even_lanes.append(jnp.where(even_lane, left, moved))
                odd_lanes.append(jnp.where(even_lane, moved, right))
            even.append(jnp.concatenate(even_lanes, axis=1))
            odd.append(jnp.concatenate(odd_lanes, axis=1))
        return jnp.concatenate(even), jnp.concatenate(odd)

    def group_step(g, by_piece, first=False):
        if not by_piece:
            for f in range(GROUP):
                frame_copy(g * GROUP + f).wait()
        for p in range(pieces):
            if by_piece:
                for copy in piece_copies(g, p):
                    copy.wait()
                start(g * pieces + p + AHEAD)
            totals = [None, None]
            for near in range(edges[p], edges[p + 1], NEAR):
                at = slice(near, near + NEAR)
                if first:
                    weigh(at)
                for parity, values in enumerate(parted(g, near)):
                    product = lax.dot_general(
                        weights[parity, :, at], values, (((1,), (1,)), ((), ())), preferred_element_type=jnp.float32
                    )
                    totals[parity] = product if totals[parity] is None else totals[parity] + product
            for parity in range(2):
                if p == 0:
                    added[parity] = totals[parity]
                else:
                    added[parity] += totals[parity]
        for parity in range(2):
            for k in range(TAPS):
                for tile in range(tiles):
                    lanes = slice(tile * LANES, (tile + 1) * LANES)
                    to = g * tiles + k // 2 + tile
                    sums[parity, k % 2, to] += added[parity, k * kept : (k + 1) * kept, lanes]
                    slab = added[parity, pl.ds(TAPS * kept + k // SUBLANES * SUBLANES, SUBLANES), lanes]
                    middle[parity, k % 2, to] += jnp.where(sublane == k % SUBLANES, slab, 0.0)

    for g in range(BY_PIECE):
        group_step(g, True, g == 0)
    for step in range(BY_PIECE * pieces + AHEAD, BY_PIECE * pieces + frames - BY_PIECE * GROUP):
        start(step)

    def later_step(g, carry):
        group_step(g, False)
        return carry

    lax.fori_loop(BY_PIECE, groups, later_step, 0)

    low = lax.broadcasted_iota(jnp.int32, (1, LANES), 1) < LANES // 2

    def joined(ref, parity):
        earlier = None
        for tile in range(ref.shape[2]):
            later = pltpu.roll(ref[parity, 1, tile], LANES // 2, 1)
            yield ref[parity, 0, tile] + jnp.where(low, 0.0 if earlier is None else earlier, later)
            earlier = later

    rows = {name: [] for name in range(4)}
    both = [joined(sums, 0), joined(sums, 1), joined(middle, 0), joined(middle, 1)]
    for tile, (e, o, e_mid, o_mid) in enumerate(zip(*both)):
        e_re, e_im, o_re, o_im = e[:half], e[half:], o[:half], o[half:]
        for name, value in enumerate((e_re + o_im, e_im - o_re, e_re - o_im, -e_im - o_re)):
            rows[name].append(value)
        centre[tile : tile + 1, :] = jnp.sum(e_mid, axis=0, keepdims=True)
        centre[2 * half_rows + tile : 2 * half_rows + tile + 1, :] = -jnp.sum(o_mid, axis=0, keepdims=True)
    for name in range(4):
        values = rows[name] + [jnp.zeros((half, LANES), jnp.float32)] * (2 * half_rows - len(rows[name]))
        part = pl.ds(2 * half_rows * (name % 2), 2 * half_rows)
        for first in range(0, half, SUBLANES):
            turned = jnp.swapaxes(jnp.stack([v[first : first + SUBLANES] for v in values]), 0, 1).astype(jnp.bfloat16)
            for i in range(SUBLANES):
                h = first + i + 1
                if name >= 2:
                    out[half - h, part] = turned[i]
                elif h < half:
                    out[half + h, part] = turned[i]
    out[half] = centre[...].astype(jnp.bfloat16)


def block_spectra(samples, kept):
    inputs, count = samples.shape
    frames = count // FRAME
    half_rows = frames * inputs // LANES
    table = tables(kept)
    rows = TAPS * kept + 2 * SUBLANES
    tiles = (frames + TAPS) * inputs // LANES
    any_spec = pl.BlockSpec(memory_space=pl.ANY)
    return pl.pallas_call(
        functools.partial(spectra_kernel, kept, frames, inputs),
        out_shape=jax.ShapeDtypeStruct((kept, 4 * half_rows, LANES), jnp.bfloat16),
        in_specs=[any_spec] * 2,
        out_specs=pl.BlockSpec(memory_space=pltpu.VMEM),
        scratch_shapes=[
            pltpu.VMEM((frames, inputs, FRAME), jnp.bfloat16),
            pltpu.VMEM(table.shape, jnp.float32),
            pltpu.VMEM((2, rows, FRAME // 2), jnp.bfloat16),
            pltpu.VMEM((2, rows, GROUP * inputs), jnp.float32),
            pltpu.VMEM((2, 2, tiles, kept, LANES), jnp.float32),
            pltpu.VMEM((2, 2, tiles, SUBLANES, LANES), jnp.float32),
            pltpu.VMEM((4 * half_rows, LANES), jnp.float32),
            pltpu.SemaphoreType.DMA((BY_PIECE * len(PIECES), GROUP + 1)),
            pltpu.SemaphoreType.DMA((frames,)),
        ],
        compiler_params=pltpu.CompilerParams(vmem_limit_bytes=(52 if rows <= 512 else 63) << 20),
    )(samples, table)


def correlate_kernel(stations, time_blocks, half_rows, scaling, arrived, out, spectra, held, sem):
    inputs = stations * LANES // 2
    low = lax.broadcasted_iota(jnp.int32, (1, LANES), 1) < LANES // 2

    def own(station, part):
        rows = []
        for z in range(time_blocks):
            here = arrived[station * time_blocks + z, 2 * half_rows * part : 2 * half_rows * (part + 1)]
            total = here[:half_rows].astype(jnp.float32)
            if z > 0:
                total += last[half_rows:].astype(jnp.float32)
            last = here
            rows.append(total)
        return jnp.concatenate(rows)

    for pair in range(stations // 2):
        parts = []
        for part in range(2):
            first, second = own(2 * pair, part), own(2 * pair + 1, part)
            parts.append(
                jnp.concatenate(
                    [
                        jnp.where(low, first, pltpu.roll(second, LANES // 2, 1)),
                        jnp.where(low, pltpu.roll(first, LANES // 2, 1), second),
                    ]
                )
            )
        lanes = slice(pair * LANES, (pair + 1) * LANES)
        spectra[:, lanes] = jnp.concatenate(parts).astype(jnp.bfloat16)
        spectra[:, inputs + pair * LANES : inputs + (pair + 1) * LANES] = jnp.concatenate(
            [parts[1], -parts[0]]
        ).astype(jnp.bfloat16)

    size = min(CORRELATED, inputs)
    copies = []
    for part in range(2):
        for begin in range(0, inputs, size):
            rows = slice(begin, begin + size)
            held[part, rows] = scaling * lax.dot_general(
                spectra[:, part * inputs + begin : part * inputs + begin + size],
                spectra[:, :inputs],
                (((0,), (0,)), ((), ())),
                preferred_element_type=jnp.float32,
            )
            copy = pltpu.make_async_copy(held.at[part, rows], out.at[0, part, rows], sem.at[len(copies)])
            copy.start()
            copies.append(copy)
    for copy in copies:
        copy.wait()


def correlate(arrived, stations, time_blocks):
    sources, rows, _ = arrived.shape
    half_rows = rows // 4
    inputs = stations * LANES // 2
    frames = time_blocks * half_rows * 2
    return pl.pallas_call(
        functools.partial(correlate_kernel, stations, time_blocks, half_rows, 1.0 / frames),
        out_shape=jax.ShapeDtypeStruct((CH_DEV, 2, inputs, inputs), jnp.float32),
        in_specs=[pl.BlockSpec(memory_space=pltpu.VMEM)],
        out_specs=pl.BlockSpec(memory_space=pl.ANY),
        scratch_shapes=[
            pltpu.VMEM((2 * frames, 2 * inputs), jnp.bfloat16),
            pltpu.VMEM((2, inputs, inputs), jnp.float32),
            pltpu.SemaphoreType.DMA((2 * inputs // min(CORRELATED, inputs),)),
        ],
        compiler_params=pltpu.CompilerParams(vmem_limit_bytes=32 << 20),
    )(arrived)


def on_device(samples):
    stations = lax.axis_size("stn")
    time_blocks = lax.axis_size("tm")
    kept = CH_DEV * stations * time_blocks
    partial = block_spectra(samples, kept)
    arrived = lax.all_to_all(partial, ("stn", "tm"), split_axis=0, concat_axis=0, tiled=True)
    return correlate(arrived, stations, time_blocks)


def solution(mesh):
    return jax.shard_map(
        on_device,
        mesh=mesh,
        in_specs=(P("stn", "tm"),),
        out_specs=P(("stn", "tm"), None, None, None),
        check_vma=False,
    )
```
